32 devices in a mesh: groups: 2 (over x), frame: 16 (over z, y, core).
Axes of the slice: x: 2, y: 2, z: 4, core: 2. Of those that a mesh axis runs over, the one named last changes fastest.
Arguments:
- frames_in: bfloat16 [32, 256, 2240], P(('groups', 'frame')), parts along dimension 0, may hold values from -16 to 16
- qkv_weight: bfloat16 [3, 2240, 1280], P(None, None, 'frame'), may hold values from -0.125 to 0.125
Outputs:
- attended: bfloat16 [32, 256, 1280], P(('groups', 'frame')), parts along dimension 0
The draws below stay inside these ranges and needn't reach their ends.
There are 2 independent parts, one for each index of `groups`. The reference program is written for one: setup_inputs(seed, part) draws one part's arguments, and reference() takes and returns one part's arrays. A program takes and returns all parts, laid end to end along the dimension named above; an argument that names none is the same for every part. Nothing has to cross between parts.
All inputs are finite; a program needn't handle non-finite values.
Results may differ from the reference program's by a relative error of at most 0.0039.
Values may be sent and summed in bfloat16 or wider, within the bound.
A program may use at most 128 MiB of HBM per device.

```python
import math
import jax
import jax.numpy as jnp
from jax import lax

D = 2240
HEAD_DIM = 32
HEADS = 40
FH = 8
FW = 32
HD = 1280
FRAMES = 16


def draw_frames_in(key, part):
    key_shared, key_frame, key_token = jax.random.split(jax.random.fold_in(key, 11), 3)
    shared = jax.random.normal(key_shared, (1, 1, D), jnp.float32) * 0.7
    frame_part = jax.random.normal(key_frame, (FRAMES, 1, D), jnp.float32) * 0.7
    token_part = jax.random.normal(key_token, (FRAMES, FH * FW, D), jnp.float32)
    position = jnp.arange(FRAMES, dtype=jnp.float32) / max(FRAMES - 1, 1)
    rising = jnp.exp(position * math.log(3.0))[:, None, None]
    values = jnp.clip(rising * (shared + frame_part + token_part), -16.0, 16.0)
    return values.astype(jnp.bfloat16)


def levels(own_key, dims, cuts, low, largest):
    factor_of = 1.0
    for axis_at, blocks in cuts:
        steps = jax.random.uniform(jax.random.fold_in(jax.random.fold_in(own_key, 6), axis_at), (blocks,), jnp.float32, low / len(cuts), largest / len(cuts))
        factor_of = factor_of * jnp.repeat(jnp.exp(steps), dims[axis_at] // blocks).reshape((-1,) + (1,) * (len(dims) - 1 - axis_at))
    return factor_of


def noise(rng, extent, deviation, bound, shards=(), kind=jnp.bfloat16):
    values = deviation * jax.random.normal(rng, extent, jnp.float32)
    if shards:
        values = values * levels(rng, extent, shards, -0.22, 0.18)
    return jnp.clip(values, -bound, bound).astype(kind)


def setup_inputs(seed: int = 0, part: int = 0) -> dict:
    seeds = jax.random.split(jax.random.key(seed), 3)
    part_splits = jax.random.split(jax.random.fold_in(seeds[2], part), 3)
    return {
        "frames_in": draw_frames_in(jax.random.fold_in(jax.random.fold_in(seeds[2], part), 71), part),
        "qkv_weight": noise(seeds[1], (3, D, HD), D ** -0.5, 0.125, ((2, 16),)),
    }


EPSILON = 1e-6


def reference(frames_in, qkv_weight):
    def frame_step(carry, frame):
        prior_state, prior_keys = carry
        queries = jnp.dot(frame, qkv_weight[0], preferred_element_type=jnp.float32)
        key_rows = jnp.dot(frame, qkv_weight[1], preferred_element_type=jnp.float32).astype(jnp.bfloat16)
        value_rows = jnp.dot(frame, qkv_weight[2], preferred_element_type=jnp.float32).astype(jnp.bfloat16)
        feature_k = jax.nn.relu(key_rows).astype(jnp.float32).reshape(-1, HEADS, HEAD_DIM)
        values = value_rows.astype(jnp.float32).reshape(-1, HEADS, HEAD_DIM)
        local_state = jnp.einsum("thi,thj->hij", feature_k, values, precision=lax.Precision.HIGHEST)
        local_keys = jnp.sum(feature_k, axis=0)
        total_state = prior_state + local_state
        total_keys = prior_keys + local_keys
        feature_q = jax.nn.relu(queries).reshape(-1, HEADS, HEAD_DIM)
        numer = jnp.einsum("thi,hij->thj", feature_q, total_state, precision=lax.Precision.HIGHEST)
        denom = jnp.einsum("thi,hi->th", feature_q, total_keys, precision=lax.Precision.HIGHEST)
        result = (numer / (denom[:, :, None] + EPSILON)).astype(jnp.bfloat16)
        return (total_state, total_keys), result.reshape(-1, HEADS * HEAD_DIM)

    start_state = jnp.zeros((HEADS, HEAD_DIM, HEAD_DIM), jnp.float32)
    start_keys = jnp.zeros((HEADS, HEAD_DIM), jnp.float32)
    final_carry, outputs = lax.scan(frame_step, (start_state, start_keys), frames_in)
    return outputs
```

```python
import functools

import jax
import jax.numpy as jnp
from jax import lax
from jax.experimental import pallas as pl
from jax.experimental.pallas import tpu as pltpu
from jax.sharding import PartitionSpec as P

HEAD_DIM = 32
HEADS = 40


EPSILON = 1e-06


def entering(shard, axis, join, neutral):
    place = lax.axis_index(axis)
    gathered = jax.tree.map(
        lambda a, kind: lax.all_gather(a.astype(kind), axis), shard, (jnp.bfloat16, jnp.bfloat16)
    )
    state = jax.tree.map(lambda a, e: jnp.zeros_like(a) + jnp.asarray(e, a.dtype), shard, neutral)

    def one(hop, state):
        return join(
            state,
            jax.tree.map(
                lambda a, own: lax.dynamic_index_in_dim(a, hop, 0, False).astype(own.dtype),
                gathered,
                shard,
            ),
        )

    return lax.fori_loop(0, place, one, state)


def add_pair(earlier, later):
    return (earlier[0] + later[0], earlier[1] + later[1])


def carry_states(key_rows, value_rows):
    count = key_rows.shape[0]
    feature_k = jax.nn.relu(key_rows).reshape(count, HEADS, HEAD_DIM)
    values = value_rows.reshape(count, HEADS, HEAD_DIM)
    local_state = jnp.einsum("thi,thj->hij", feature_k, values, preferred_element_type=jnp.float32)
    local_keys = jnp.sum(feature_k.astype(jnp.float32), axis=0)
    prior_state, prior_keys = entering(
        (local_state, local_keys),
        "frame",
        add_pair,
        (jnp.zeros_like(local_state), jnp.zeros_like(local_keys)),
    )
    return (local_state, local_keys, prior_state, prior_keys)


def apply_state(feature_q, state, key_sum):
    numer = jnp.einsum("thi,hij->thj", feature_q, state, precision=lax.Precision.HIGHEST)
    denom = jnp.einsum("thi,hi->th", feature_q, key_sum, precision=lax.Precision.HIGHEST)
    return (numer, denom)


def gathered_shards(frames_in, qkv_weight):
    tokens = frames_in[0]
    count = tokens.shape[0]
    weights_all = lax.all_gather(qkv_weight, "frame", axis=2, tiled=True)
    projected = jnp.einsum("td,sdc->stc", tokens, weights_all, preferred_element_type=jnp.float32)
    queries = projected[0]
    key_rows = projected[1].astype(jnp.bfloat16)
    value_rows = projected[2].astype(jnp.bfloat16)
    local_state, local_keys, prior_state, prior_keys = carry_states(key_rows, value_rows)
    feature_q = jax.nn.relu(queries).reshape(count, HEADS, HEAD_DIM)
    own_numer, own_denom = apply_state(feature_q, local_state, local_keys)
    past_numer, past_denom = apply_state(feature_q, prior_state, prior_keys)
    numer = past_numer + own_numer
    denom = past_denom + own_denom
    attended = (numer / (denom[:, :, None] + EPSILON)).astype(jnp.bfloat16)
    return attended.reshape(1, count, HEADS * HEAD_DIM)


K, V, Q = 0, 1, 2
KIND_AT = (1, 2, 0)


def kernel(
    lines, x_in, w_in, out, wbuf, xbuf, obuf, st, sib, total, pre, chain,
    w_recv, z_send, x_send, d_send, own_sem, fx_local, fx_send, fx_recv,
    s_send, s_recv, c_send, c_recv, o_local, o_send, o_recv,
):
    half_rows = w_in.shape[1]
    rows = 2 * half_rows
    group_heads = rows // HEAD_DIM
    bf16, f32 = jnp.bfloat16, jnp.float32

    x = lax.axis_index("groups")
    f = lax.axis_index("frame")
    z, y, c = f // 4, (f // 2) % 2, f % 2
    primary = c == x
    first, last = z == 0, z == lines - 1

    def place(x, z, y, c):
        return {"groups": x, "frame": z * 4 + y * 2 + c}

    left, right = place(x, z - 1, y, c), place(x, z + 1, y, c)
    sibling, across, facing = place(x, z, y, 1 - c), place(1 - x, z, y, c), place(x, z, 1 - y, c)

    inner = jnp.where((z == 0) | (z == lines - 1), 0, 1)
    low = z < 2
    order = [z]
    for k in (1, 2, 3):
        end = jnp.where(low, k, 3 - k)
        mid = jnp.where(low, (1, 0, 2, 3)[k], (2, 3, 1, 0)[k])
        order.append(jnp.where(inner == 1, mid, end))

    def block(kind, g, h):
        return wbuf.at[g, pl.ds(pl.multiple_of(kind * rows + h * half_rows, 16), half_rows), :]

    def w_copy(src, kind, g, send, to):
        return pltpu.make_async_remote_copy(
            src_ref=src, dst_ref=block(kind, g, c), send_sem=send,
            recv_sem=w_recv.at[kind, g, c], device_id=to, device_id_type=pl.DeviceIdType.MESH,
        )

    def w_arrived(kind, g, h):
        pltpu.make_async_copy(block(kind, g, h), block(kind, g, h), w_recv.at[kind, g, h]).wait()

    barrier = pltpu.get_barrier_semaphore()

    def greet(who):
        pl.semaphore_signal(barrier, inc=1, device_id=who, device_id_type=pl.DeviceIdType.MESH)

    greet(sibling)
    greet(across)
    greet(facing)

    @pl.when(jnp.logical_not(first))
    def _():
        greet(left)

    @pl.when(jnp.logical_not(last))
    def _():
        greet(right)

    own_copies = [
        pltpu.make_async_copy(w_in.at[KIND_AT[kind]], block(kind, z, c), own_sem.at[kind])
        for kind in (K, V, Q)
    ]
    frame_local = pltpu.make_async_copy(x_in, xbuf.at[y], fx_local)
    frame_local.start()
    for copy in own_copies:
        copy.start()

    pl.semaphore_wait(barrier, 3 + jnp.where(first, 0, 1) + jnp.where(last, 0, 1))

    def own_z(kind, op):
        src = w_in.at[KIND_AT[kind]]

        @pl.when(primary & jnp.logical_not(first))
        def _():
            op(w_copy(src, kind, z, z_send.at[0, kind, z], left))

        @pl.when(primary & jnp.logical_not(last))
        def _():
            op(w_copy(src, kind, z, z_send.at[1, kind, z], right))

    def own_d(kind):
        return w_copy(w_in.at[KIND_AT[kind]], kind, z, d_send.at[kind, z], sibling)

    def forward(kind, g, op):
        src = block(kind, g, c)

        @pl.when(primary & (g > z) & jnp.logical_not(first))
        def _():
            op(w_copy(src, kind, g, z_send.at[0, kind, g], left))

        @pl.when(primary & (g < z) & jnp.logical_not(last))
        def _():
            op(w_copy(src, kind, g, z_send.at[1, kind, g], right))

        @pl.when(primary)
        def _():
            op(w_copy(src, kind, g, x_send.at[kind, g], across))

        op(w_copy(src, kind, g, d_send.at[kind, g], sibling))

    start = lambda copy: copy.start()
    sent = lambda copy: copy.wait_send()

    own_z(K, start)
    own_z(V, start)
    frame_far = pltpu.make_async_remote_copy(
        src_ref=x_in, dst_ref=xbuf.at[y], send_sem=fx_send, recv_sem=fx_recv,
        device_id=facing, device_id_type=pl.DeviceIdType.MESH,
    )
    frame_far.start()
    for kind in (K, V, Q):
        own_d(kind).start()

    def relay(kind, g):
        w_arrived(kind, g, c)
        forward(kind, g, start)

    row_head = lax.broadcasted_iota(jnp.int32, (rows, rows), 0) // HEAD_DIM
    col_head = lax.broadcasted_iota(jnp.int32, (rows, rows), 1) // HEAD_DIM
    same_head = row_head == col_head

    def states(g, side):
        kv = jnp.dot(wbuf[g, 0 : 2 * rows, :], xbuf[side], preferred_element_type=f32)
        keys = jnp.maximum(kv[:rows].astype(bf16), jnp.zeros((), bf16))
        values = kv[rows:].astype(bf16)
        values = jnp.concatenate([values, jnp.ones((16, values.shape[1]), bf16)], axis=0)
        full = lax.dot_general(values, keys, (((1,), (1,)), ((), ())), preferred_element_type=f32)
        kept = jnp.where(same_head, full[:rows], 0.0)
        packed = kept[0:HEAD_DIM]
        for h in range(1, group_heads):
            packed = packed + kept[h * HEAD_DIM : (h + 1) * HEAD_DIM]
        st[side, g, 0:HEAD_DIM, :] = packed
        st[side, g, HEAD_DIM : HEAD_DIM + 8, :] = full[rows : rows + 8]

    def attend(g, side):
        queries = jnp.dot(wbuf[g, 2 * rows : 3 * rows, :], xbuf[side], preferred_element_type=f32)
        queries = jnp.maximum(queries, 0.0)
        q_hi = queries.astype(bf16)
        q_lo = (queries - q_hi.astype(f32)).astype(bf16)
        packed = total[side, g]
        numer = jnp.concatenate([packed[0:HEAD_DIM]] * group_heads, axis=0)
        denom = jnp.concatenate([packed[HEAD_DIM : HEAD_DIM + 8]] * (rows // 8), axis=0)
        state = jnp.concatenate(
            [jnp.where(same_head, numer, 0.0), jnp.where(same_head, denom, 0.0)], axis=0
        )
        s_hi = state.astype(bf16)
        s_lo = (state - s_hi.astype(f32)).astype(bf16)
        both = (
            jnp.dot(s_hi, q_hi, preferred_element_type=f32)
            + jnp.dot(s_hi, q_lo, preferred_element_type=f32)
            + jnp.dot(s_lo, q_hi, preferred_element_type=f32)
        )
        obuf[side, g] = (both[:rows] / (both[rows:] + EPSILON)).astype(bf16)

    def out_rows(g):
        return out.at[pl.ds(pl.multiple_of((2 * g + y) * rows, 16), rows), :]

    def out_local(g):
        return pltpu.make_async_copy(obuf.at[y, g], out_rows(g), o_local.at[g])

    def out_far(g):
        return pltpu.make_async_remote_copy(
            src_ref=obuf.at[1 - y, g], dst_ref=out_rows(g), send_sem=o_send.at[g],
            recv_sem=o_recv.at[g], device_id=facing, device_id_type=pl.DeviceIdType.MESH,
        )

    frame_local.wait()
    for copy in own_copies:
        copy.wait()

    for k in (1, 2, 3):
        for kind in (K, V):
            relay(kind, order[k])
        for kind in (K, V):
            w_arrived(kind, order[k - 1], 1 - c)
        states(order[k - 1], y)
    own_z(Q, start)
    for kind in (K, V):
        w_arrived(kind, order[3], 1 - c)
    states(order[3], y)
    frame_far.wait_recv()

    @pl.loop(0, 2)
    def _(g):
        states(g, 1 - y)

    relay(Q, order[1])

    @pl.loop(2, 4)
    def _(g):
        states(g, 1 - y)

    swap = pltpu.make_async_remote_copy(
        src_ref=st, dst_ref=sib, send_sem=s_send, recv_sem=s_recv,
        device_id=sibling, device_id_type=pl.DeviceIdType.MESH,
    )
    swap.start()
    swap.wait_recv()
    near = st[0] + sib[0]
    whole = near + st[1] + sib[1]
    later = jnp.where(c == 1, 1.0, 0.0).astype(f32)

    def onward():
        return pltpu.make_async_remote_copy(
            src_ref=chain, dst_ref=pre, send_sem=c_send, recv_sem=c_recv,
            device_id=right, device_id_type=pl.DeviceIdType.MESH,
        )

    @pl.when(first)
    def _():
        pre[...] = jnp.zeros_like(pre)

    @pl.when(jnp.logical_not(first))
    def _():
        pltpu.make_async_copy(pre, pre, c_recv).wait()

    @pl.when(jnp.logical_not(last))
    def _():
        chain[...] = pre[...] + whole
        onward().start()

    before = pre[...]
    total[0] = before + st[0] + later * sib[0]
    total[1] = before + near + st[1] + later * sib[1]

    def finish(g):
        w_arrived(Q, g, 1 - c)
        attend(g, 1 - y)
        out_far(g).start()
        attend(g, y)
        out_local(g).start()

    relay(Q, order[2])
    finish(order[0])
    relay(Q, order[3])
    for k in (1, 2, 3):
        finish(order[k])

    for kind in (K, V, Q):
        own_z(kind, sent)
        own_d(kind).wait_send()
        for k in (1, 2, 3):
            forward(kind, order[k], sent)
    frame_far.wait_send()
    swap.wait_send()

    @pl.when(jnp.logical_not(last))
    def _():
        onward().wait_send()

    for g in range(4):
        out_local(g).wait()
        out_far(g).wait_send()
    for g in range(4):
        theirs = out.at[pl.ds(pl.multiple_of((2 * g + 1 - y) * rows, 16), rows), :]
        pltpu.make_async_copy(theirs, theirs, o_recv.at[g]).wait()


def kernel_shards(lines, frames_in, qkv_weight):
    tokens = jnp.swapaxes(frames_in[0], 0, 1)
    weights = jnp.swapaxes(qkv_weight, 1, 2)
    depth, count = tokens.shape
    half_rows = weights.shape[1]
    rows = 2 * half_rows
    dma = pltpu.SemaphoreType.DMA
    bf16, f32 = jnp.bfloat16, jnp.float32
    packed = (lines, HEAD_DIM + 8, rows)
    out = pl.pallas_call(
        functools.partial(kernel, lines),
        out_shape=jax.ShapeDtypeStruct((HEADS * HEAD_DIM, count), bf16),
        in_specs=[pl.BlockSpec(memory_space=pl.ANY)] * 2,
        out_specs=pl.BlockSpec(memory_space=pl.ANY),
        scratch_shapes=[
            pltpu.VMEM((lines, 3 * rows, depth), bf16),
            pltpu.VMEM((2, depth, count), bf16),
            pltpu.VMEM((2, lines, rows, count), bf16),
            pltpu.VMEM((2,) + packed, f32),
            pltpu.VMEM((2,) + packed, f32),
            pltpu.VMEM((2,) + packed, f32),
            pltpu.VMEM(packed, f32),
            pltpu.VMEM(packed, f32),
            dma((3, lines, 2)),
            dma((2, 3, lines)),
            dma((3, lines)),
            dma((3, lines)),
            dma((3,)),
            dma, dma, dma, dma, dma, dma, dma,
            dma((lines,)),
            dma((lines,)),
            dma((lines,)),
        ],
        compiler_params=pltpu.CompilerParams(
            collective_id=0, has_side_effects=True, vmem_limit_bytes=48 * 1024 * 1024
        ),
    )(tokens, weights)
    return jnp.swapaxes(out, 0, 1)[None]


def solution(mesh):
    placed = (P(("groups", "frame"), None, None), P(None, None, "frame"))
    fits = mesh.shape["groups"] == 2 and mesh.shape["frame"] == 16
    shards = functools.partial(kernel_shards, mesh.shape["frame"] // 4) if fits else gathered_shards
    return jax.shard_map(
        shards,
        mesh=mesh,
        in_specs=placed,
        out_specs=P(("groups", "frame"), None, None),
        check_vma=False,
    )
```

```python
import functools

import jax
import jax.numpy as jnp
from jax import lax
from jax.experimental import pallas as pl
from jax.experimental.pallas import tpu as pltpu
from jax.sharding import PartitionSpec as P

HEAD_DIM = 32
HEADS = 40


EPSILON = 1e-06


def entering(shard, axis, join, neutral):
    place = lax.axis_index(axis)
    gathered = jax.tree.map(
        lambda a, kind: lax.all_gather(a.astype(kind), axis), shard, (jnp.bfloat16, jnp.bfloat16)
    )
    state = jax.tree.map(lambda a, e: jnp.zeros_like(a) + jnp.asarray(e, a.dtype), shard, neutral)

    def one(hop, state):
        return join(
            state,
            jax.tree.map(
                lambda a, own: lax.dynamic_index_in_dim(a, hop, 0, False).astype(own.dtype),
                gathered,
                shard,
            ),
        )

    return lax.fori_loop(0, place, one, state)


def add_pair(earlier, later):
    return (earlier[0] + later[0], earlier[1] + later[1])


def carry_states(key_rows, value_rows):
    count = key_rows.shape[0]
    feature_k = jax.nn.relu(key_rows).reshape(count, HEADS, HEAD_DIM)
    values = value_rows.reshape(count, HEADS, HEAD_DIM)
    local_state = jnp.einsum("thi,thj->hij", feature_k, values, preferred_element_type=jnp.float32)
    local_keys = jnp.sum(feature_k.astype(jnp.float32), axis=0)
    prior_state, prior_keys = entering(
        (local_state, local_keys),
        "frame",
        add_pair,
        (jnp.zeros_like(local_state), jnp.zeros_like(local_keys)),
    )
    return (local_state, local_keys, prior_state, prior_keys)


def apply_state(feature_q, state, key_sum):
    numer = jnp.einsum("thi,hij->thj", feature_q, state, precision=lax.Precision.HIGHEST)
    denom = jnp.einsum("thi,hi->th", feature_q, key_sum, precision=lax.Precision.HIGHEST)
    return (numer, denom)


def gathered_shards(frames_in, qkv_weight):
    tokens = frames_in[0]
    count = tokens.shape[0]
    weights_all = lax.all_gather(qkv_weight, "frame", axis=2, tiled=True)
    projected = jnp.einsum("td,sdc->stc", tokens, weights_all, preferred_element_type=jnp.float32)
    queries = projected[0]
    key_rows = projected[1].astype(jnp.bfloat16)
    value_rows = projected[2].astype(jnp.bfloat16)
    local_state, local_keys, prior_state, prior_keys = carry_states(key_rows, value_rows)
    feature_q = jax.nn.relu(queries).reshape(count, HEADS, HEAD_DIM)
    own_numer, own_denom = apply_state(feature_q, local_state, local_keys)
    past_numer, past_denom = apply_state(feature_q, prior_state, prior_keys)
    numer = past_numer + own_numer
    denom = past_denom + own_denom
    attended = (numer / (denom[:, :, None] + EPSILON)).astype(jnp.bfloat16)
    return attended.reshape(1, count, HEADS * HEAD_DIM)


K, V, Q = 0, 1, 2
KIND_AT = (1, 2, 0)


def kernel(
    lines, x_in, w_in, out, wbuf, xbuf, qbuf, obuf, st, sib, total, pre, chain,
    w_recv, z_send, x_send, d_send, own_sem, fx_local, fx_send, fx_recv,
    s_send, s_recv, c_send, c_recv, h_send, h_recv, o_local, o_send, o_recv,
):
    half_rows = w_in.shape[1]
    rows = 2 * half_rows
    group_heads = rows // HEAD_DIM
    bf16, f32 = jnp.bfloat16, jnp.float32

    x = lax.axis_index("groups")
    f = lax.axis_index("frame")
    z, y, c = f // 4, (f // 2) % 2, f % 2
    primary = c == x
    first, last = z == 0, z == lines - 1

    def place(x, z, y, c):
        return {"groups": x, "frame": z * 4 + y * 2 + c}

    left, right = place(x, z - 1, y, c), place(x, z + 1, y, c)
    sibling, across, facing = place(x, z, y, 1 - c), place(1 - x, z, y, c), place(x, z, 1 - y, c)

    inner = jnp.where((z == 0) | (z == lines - 1), 0, 1)
    low = z < 2
    order = [z]
    for k in (1, 2, 3):
        end = jnp.where(low, k, 3 - k)
        mid = jnp.where(low, (1, 0, 2, 3)[k], (2, 3, 1, 0)[k])
        order.append(jnp.where(inner == 1, mid, end))

    def block(kind, g, h):
        return wbuf.at[g, pl.ds(pl.multiple_of(kind * rows + h * half_rows, 16), half_rows), :]

    def w_copy(src, kind, g, send, to):
        return pltpu.make_async_remote_copy(
            src_ref=src, dst_ref=block(kind, g, c), send_sem=send,
            recv_sem=w_recv.at[kind, g, c], device_id=to, device_id_type=pl.DeviceIdType.MESH,
        )

    def w_arrived(kind, g, h):
        pltpu.make_async_copy(block(kind, g, h), block(kind, g, h), w_recv.at[kind, g, h]).wait()

    barrier = pltpu.get_barrier_semaphore()

    def greet(who):
        pl.semaphore_signal(barrier, inc=1, device_id=who, device_id_type=pl.DeviceIdType.MESH)

    greet(sibling)
    greet(across)
    greet(facing)

    @pl.when(jnp.logical_not(first))
    def _():
        greet(left)

    @pl.when(jnp.logical_not(last))
    def _():
        greet(right)

    own_copies = [
        pltpu.make_async_copy(w_in.at[KIND_AT[kind]], block(kind, z, c), own_sem.at[kind])
        for kind in (K, V, Q)
    ]
    frame_local = pltpu.make_async_copy(x_in, xbuf.at[y], fx_local)
    frame_local.start()
    for copy in own_copies:
        copy.start()

    pl.semaphore_wait(barrier, 3 + jnp.where(first, 0, 1) + jnp.where(last, 0, 1))

    def own_z(kind, op):
        src = w_in.at[KIND_AT[kind]]

        @pl.when(primary & jnp.logical_not(first))
        def _():
            op(w_copy(src, kind, z, z_send.at[0, kind, z], left))

        @pl.when(primary & jnp.logical_not(last))
        def _():
            op(w_copy(src, kind, z, z_send.at[1, kind, z], right))

    def own_d(kind):
        return w_copy(w_in.at[KIND_AT[kind]], kind, z, d_send.at[kind, z], sibling)

    def forward(kind, g, op):
        src = block(kind, g, c)

        @pl.when(primary & (g > z) & jnp.logical_not(first))
        def _():
            op(w_copy(src, kind, g, z_send.at[0, kind, g], left))

        @pl.when(primary & (g < z) & jnp.logical_not(last))
        def _():
            op(w_copy(src, kind, g, z_send.at[1, kind, g], right))

        @pl.when(primary)
        def _():
            op(w_copy(src, kind, g, x_send.at[kind, g], across))

        op(w_copy(src, kind, g, d_send.at[kind, g], sibling))

    start = lambda copy: copy.start()
    sent = lambda copy: copy.wait_send()

    own_z(K, start)
    own_z(V, start)
    frame_far = pltpu.make_async_remote_copy(
        src_ref=x_in, dst_ref=xbuf.at[y], send_sem=fx_send, recv_sem=fx_recv,
        device_id=facing, device_id_type=pl.DeviceIdType.MESH,
    )
    frame_far.start()
    for kind in (K, V, Q):
        own_d(kind).start()

    def relay(kind, g):
        w_arrived(kind, g, c)
        forward(kind, g, start)

    row_head = lax.broadcasted_iota(jnp.int32, (rows, rows), 0) // HEAD_DIM
    col_head = lax.broadcasted_iota(jnp.int32, (rows, rows), 1) // HEAD_DIM
    same_head = row_head == col_head

    def states(g, side):
        kv = jnp.dot(wbuf[g, 0 : 2 * rows, :], xbuf[side], preferred_element_type=f32)
        keys = jnp.maximum(kv[:rows].astype(bf16), jnp.zeros((), bf16))
        values = kv[rows:].astype(bf16)
        values = jnp.concatenate([values, jnp.ones((16, values.shape[1]), bf16)], axis=0)
        full = lax.dot_general(values, keys, (((1,), (1,)), ((), ())), preferred_element_type=f32)
        kept = jnp.where(same_head, full[:rows], 0.0)
        packed = kept[0:HEAD_DIM]
        for h in range(1, group_heads):
            packed = packed + kept[h * HEAD_DIM : (h + 1) * HEAD_DIM]
        st[side, g, 0:HEAD_DIM, :] = packed
        st[side, g, HEAD_DIM : HEAD_DIM + 8, :] = full[rows : rows + 8]

    def project(g, side):
        queries = jnp.dot(wbuf[g, 2 * rows : 3 * rows, :], xbuf[side], preferred_element_type=f32)
        qbuf[side, g] = jnp.maximum(queries, 0.0)

    def attend(g, side):
        queries = qbuf[side, g]
        q_hi = queries.astype(bf16)
        q_lo = (queries - q_hi.astype(f32)).astype(bf16)
        packed = total[side, g]
        numer = jnp.concatenate([packed[0:HEAD_DIM]] * group_heads, axis=0)
        denom = jnp.concatenate([packed[HEAD_DIM : HEAD_DIM + 8]] * (rows // 8), axis=0)
        state = jnp.concatenate(
            [jnp.where(same_head, numer, 0.0), jnp.where(same_head, denom, 0.0)], axis=0
        )
        s_hi = state.astype(bf16)
        s_lo = (state - s_hi.astype(f32)).astype(bf16)
        both = (
            jnp.dot(s_hi, q_hi, preferred_element_type=f32)
            + jnp.dot(s_hi, q_lo, preferred_element_type=f32)
            + jnp.dot(s_lo, q_hi, preferred_element_type=f32)
        )
        obuf[side, g] = (both[:rows] / (both[rows:] + EPSILON)).astype(bf16)

    def out_rows(g):
        return out.at[pl.ds(pl.multiple_of((2 * g + y) * rows, 16), rows), :]

    def out_local(g):
        return pltpu.make_async_copy(obuf.at[y, g], out_rows(g), o_local.at[g])

    def out_far(g):
        return pltpu.make_async_remote_copy(
            src_ref=obuf.at[1 - y, g], dst_ref=out_rows(g), send_sem=o_send.at[g],
            recv_sem=o_recv.at[g], device_id=facing, device_id_type=pl.DeviceIdType.MESH,
        )

    frame_local.wait()
    for copy in own_copies:
        copy.wait()

    for k in (1, 2, 3):
        for kind in (K, V):
            relay(kind, order[k])
        for kind in (K, V):
            w_arrived(kind, order[k - 1], 1 - c)
        states(order[k - 1], y)
    own_z(Q, start)
    for kind in (K, V):
        w_arrived(kind, order[3], 1 - c)
    states(order[3], y)
    relay(Q, order[1])
    frame_far.wait_recv()

    @pl.loop(0, 4)
    def _(g):
        states(g, 1 - y)

    swap = pltpu.make_async_remote_copy(
        src_ref=st, dst_ref=sib, send_sem=s_send, recv_sem=s_recv,
        device_id=sibling, device_id_type=pl.DeviceIdType.MESH,
    )
    swap.start()
    relay(Q, order[2])

    mine = pl.ds(2 * c, 2)
    onward = pltpu.make_async_remote_copy(
        src_ref=chain.at[mine], dst_ref=pre.at[mine], send_sem=c_send, recv_sem=c_recv,
        device_id=right, device_id_type=pl.DeviceIdType.MESH,
    )
    share = pltpu.make_async_remote_copy(
        src_ref=pre.at[mine], dst_ref=pre.at[mine], send_sem=h_send, recv_sem=h_recv,
        device_id=sibling, device_id_type=pl.DeviceIdType.MESH,
    )
    swap.wait_recv()
    near = st[0] + sib[0]
    later = jnp.where(c == 1, 1.0, 0.0).astype(f32)
    total[0] = st[0] + later * sib[0]
    total[1] = near + st[1] + later * sib[1]
    chain[...] = near + st[1] + sib[1]

    @pl.when(first)
    def _():
        onward.start()

    def project_both(g):
        w_arrived(Q, g, 1 - c)

        @pl.loop(0, 2)
        def _(side):
            project(g, side)

    project_both(order[0])
    relay(Q, order[3])

    @pl.when(jnp.logical_not(first))
    def _():
        pltpu.make_async_copy(pre.at[mine], pre.at[mine], c_recv).wait()

        @pl.when(jnp.logical_not(last))
        def _():
            chain[mine] = chain[mine] + pre[mine]
            onward.start()

        share.start()

    for k in (1, 2):
        project_both(order[k])

    @pl.when(jnp.logical_not(first))
    def _():
        share.wait_recv()
        total[0] = total[0] + pre[...]
        total[1] = total[1] + pre[...]

    def finish(g):
        attend(g, 1 - y)
        out_far(g).start()
        attend(g, y)
        out_local(g).start()

    for k in (0, 1, 2):
        finish(order[k])
    project_both(order[3])
    finish(order[3])

    for kind in (K, V, Q):
        own_z(kind, sent)
        own_d(kind).wait_send()
        for k in (1, 2, 3):
            forward(kind, order[k], sent)
    frame_far.wait_send()
    swap.wait_send()

    @pl.when(jnp.logical_not(first))
    def _():
        share.wait_send()

    @pl.when(jnp.logical_not(last))
    def _():
        onward.wait_send()

    for g in range(4):
        out_local(g).wait()
        out_far(g).wait_send()
    for g in range(4):
        theirs = out.at[pl.ds(pl.multiple_of((2 * g + 1 - y) * rows, 16), rows), :]
        pltpu.make_async_copy(theirs, theirs, o_recv.at[g]).wait()


def kernel_shards(lines, frames_in, qkv_weight):
    tokens = jnp.swapaxes(frames_in[0], 0, 1)
    weights = jnp.swapaxes(qkv_weight, 1, 2)
    depth, count = tokens.shape
    half_rows = weights.shape[1]
    rows = 2 * half_rows
    dma = pltpu.SemaphoreType.DMA
    bf16, f32 = jnp.bfloat16, jnp.float32
    packed = (lines, HEAD_DIM + 8, rows)
    out = pl.pallas_call(
        functools.partial(kernel, lines),
        out_shape=jax.ShapeDtypeStruct((HEADS * HEAD_DIM, count), bf16),
        in_specs=[pl.BlockSpec(memory_space=pl.ANY)] * 2,
        out_specs=pl.BlockSpec(memory_space=pl.ANY),
        scratch_shapes=[
            pltpu.VMEM((lines, 3 * rows, depth), bf16),
            pltpu.VMEM((2, depth, count), bf16),
            pltpu.VMEM((2, lines, rows, count), f32),
            pltpu.VMEM((2, lines, rows, count), bf16),
            pltpu.VMEM((2,) + packed, f32),
            pltpu.VMEM((2,) + packed, f32),
            pltpu.VMEM((2,) + packed, f32),
            pltpu.VMEM(packed, f32),
            pltpu.VMEM(packed, f32),
            dma((3, lines, 2)),
            dma((2, 3, lines)),
            dma((3, lines)),
            dma((3, lines)),
            dma((3,)),
            dma, dma, dma, dma, dma, dma, dma, dma, dma,
            dma((lines,)),
            dma((lines,)),
            dma((lines,)),
        ],
        compiler_params=pltpu.CompilerParams(
            collective_id=0, has_side_effects=True, vmem_limit_bytes=63 * 1024 * 1024
        ),
    )(tokens, weights)
    return jnp.swapaxes(out, 0, 1)[None]


def solution(mesh):
    placed = (P(("groups", "frame"), None, None), P(None, None, "frame"))
    fits = mesh.shape["groups"] == 2 and mesh.shape["frame"] == 16
    shards = functools.partial(kernel_shards, mesh.shape["frame"] // 4) if fits else gathered_shards
    return jax.shard_map(
        shards,
        mesh=mesh,
        in_specs=placed,
        out_specs=P(("groups", "frame"), None, None),
        check_vma=False,
    )
```

```python
import functools

import jax
import jax.numpy as jnp
from jax import lax
from jax.experimental import pallas as pl
from jax.experimental.pallas import tpu as pltpu
from jax.sharding import PartitionSpec as P

HEAD_DIM = 32
HEADS = 40


EPSILON = 1e-06


def entering(shard, axis, join, neutral):
    place = lax.axis_index(axis)
    gathered = jax.tree.map(
        lambda a, kind: lax.all_gather(a.astype(kind), axis), shard, (jnp.bfloat16, jnp.bfloat16)
    )
    state = jax.tree.map(lambda a, e: jnp.zeros_like(a) + jnp.asarray(e, a.dtype), shard, neutral)

    def one(hop, state):
        return join(
            state,
            jax.tree.map(
                lambda a, own: lax.dynamic_index_in_dim(a, hop, 0, False).astype(own.dtype),
                gathered,
                shard,
            ),
        )

    return lax.fori_loop(0, place, one, state)


def add_pair(earlier, later):
    return (earlier[0] + later[0], earlier[1] + later[1])


def carry_states(key_rows, value_rows):
    count = key_rows.shape[0]
    feature_k = jax.nn.relu(key_rows).reshape(count, HEADS, HEAD_DIM)
    values = value_rows.reshape(count, HEADS, HEAD_DIM)
    local_state = jnp.einsum("thi,thj->hij", feature_k, values, preferred_element_type=jnp.float32)
    local_keys = jnp.sum(feature_k.astype(jnp.float32), axis=0)
    prior_state, prior_keys = entering(
        (local_state, local_keys),
        "frame",
        add_pair,
        (jnp.zeros_like(local_state), jnp.zeros_like(local_keys)),
    )
    return (local_state, local_keys, prior_state, prior_keys)


def apply_state(feature_q, state, key_sum):
    numer = jnp.einsum("thi,hij->thj", feature_q, state, precision=lax.Precision.HIGHEST)
    denom = jnp.einsum("thi,hi->th", feature_q, key_sum, precision=lax.Precision.HIGHEST)
    return (numer, denom)


def gathered_shards(frames_in, qkv_weight):
    tokens = frames_in[0]
    count = tokens.shape[0]
    weights_all = lax.all_gather(qkv_weight, "frame", axis=2, tiled=True)
    projected = jnp.einsum("td,sdc->stc", tokens, weights_all, preferred_element_type=jnp.float32)
    queries = projected[0]
    key_rows = projected[1].astype(jnp.bfloat16)
    value_rows = projected[2].astype(jnp.bfloat16)
    local_state, local_keys, prior_state, prior_keys = carry_states(key_rows, value_rows)
    feature_q = jax.nn.relu(queries).reshape(count, HEADS, HEAD_DIM)
    own_numer, own_denom = apply_state(feature_q, local_state, local_keys)
    past_numer, past_denom = apply_state(feature_q, prior_state, prior_keys)
    numer = past_numer + own_numer
    denom = past_denom + own_denom
    attended = (numer / (denom[:, :, None] + EPSILON)).astype(jnp.bfloat16)
    return attended.reshape(1, count, HEADS * HEAD_DIM)


K, V, Q = 0, 1, 2
KIND_AT = (1, 2, 0)


def kernel(
    lines, x_in, w_in, out, wbuf, xbuf, qbuf, obuf, st, sib, total, pre, chain,
    w_recv, z_send, x_send, d_send, own_sem, fx_local, fx_send, fx_recv,
    s_send, s_recv, c_send, c_recv, h_send, h_recv, o_local, o_send, o_recv,
):
    half_rows = w_in.shape[1]
    rows = 2 * half_rows
    group_heads = rows // HEAD_DIM
    bf16, f32 = jnp.bfloat16, jnp.float32

    x = lax.axis_index("groups")
    f = lax.axis_index("frame")
    z, y, c = f // 4, (f // 2) % 2, f % 2
    primary = c == x
    first, last = z == 0, z == lines - 1

    def place(x, z, y, c):
        return {"groups": x, "frame": z * 4 + y * 2 + c}

    left, right = place(x, z - 1, y, c), place(x, z + 1, y, c)
    sibling, across, facing = place(x, z, y, 1 - c), place(1 - x, z, y, c), place(x, z, 1 - y, c)

    inner = jnp.where((z == 0) | (z == lines - 1), 0, 1)
    low = z < 2
    order = [z]
    for k in (1, 2, 3):
        end = jnp.where(low, k, 3 - k)
        mid = jnp.where(low, (1, 0, 2, 3)[k], (2, 3, 1, 0)[k])
        order.append(jnp.where(inner == 1, mid, end))

    def block(kind, g, h):
        return wbuf.at[g, pl.ds(pl.multiple_of(kind * rows + h * half_rows, 16), half_rows), :]

    def w_copy(src, kind, g, send, to):
        return pltpu.make_async_remote_copy(
            src_ref=src, dst_ref=block(kind, g, c), send_sem=send,
            recv_sem=w_recv.at[kind, g, c], device_id=to, device_id_type=pl.DeviceIdType.MESH,
        )

    def w_arrived(kind, g, h):
        pltpu.make_async_copy(block(kind, g, h), block(kind, g, h), w_recv.at[kind, g, h]).wait()

    barrier = pltpu.get_barrier_semaphore()

    def greet(who):
        pl.semaphore_signal(barrier, inc=1, device_id=who, device_id_type=pl.DeviceIdType.MESH)

    greet(sibling)
    greet(across)
    greet(facing)

    @pl.when(jnp.logical_not(first))
    def _():
        greet(left)

    @pl.when(jnp.logical_not(last))
    def _():
        greet(right)

    own_copies = [
        pltpu.make_async_copy(w_in.at[KIND_AT[kind]], block(kind, z, c), own_sem.at[kind])
        for kind in (K, V, Q)
    ]
    frame_local = pltpu.make_async_copy(x_in, xbuf.at[y], fx_local)
    frame_local.start()
    for copy in own_copies:
        copy.start()

    pl.semaphore_wait(barrier, 3 + jnp.where(first, 0, 1) + jnp.where(last, 0, 1))

    def own_z(kind, op):
        src = w_in.at[KIND_AT[kind]]

        @pl.when(primary & jnp.logical_not(first))
        def _():
            op(w_copy(src, kind, z, z_send.at[0, kind, z], left))

        @pl.when(primary & jnp.logical_not(last))
        def _():
            op(w_copy(src, kind, z, z_send.at[1, kind, z], right))

    def own_d(kind):
        return w_copy(w_in.at[KIND_AT[kind]], kind, z, d_send.at[kind, z], sibling)

    def forward(kind, g, op):
        src = block(kind, g, c)

        @pl.when(primary & (g > z) & jnp.logical_not(first))
        def _():
            op(w_copy(src, kind, g, z_send.at[0, kind, g], left))

        @pl.when(primary & (g < z) & jnp.logical_not(last))
        def _():
            op(w_copy(src, kind, g, z_send.at[1, kind, g], right))

        @pl.when(primary)
        def _():
            op(w_copy(src, kind, g, x_send.at[kind, g], across))

        op(w_copy(src, kind, g, d_send.at[kind, g], sibling))

    start = lambda copy: copy.start()
    sent = lambda copy: copy.wait_send()

    own_z(K, start)
    own_z(V, start)
    frame_far = pltpu.make_async_remote_copy(
        src_ref=x_in, dst_ref=xbuf.at[y], send_sem=fx_send, recv_sem=fx_recv,
        device_id=facing, device_id_type=pl.DeviceIdType.MESH,
    )
    frame_far.start()
    for kind in (K, V, Q):
        own_d(kind).start()

    def relay(kind, g):
        w_arrived(kind, g, c)
        forward(kind, g, start)

    row_head = lax.broadcasted_iota(jnp.int32, (rows, rows), 0) // HEAD_DIM
    col_head = lax.broadcasted_iota(jnp.int32, (rows, rows), 1) // HEAD_DIM
    same_head = row_head == col_head

    def states(g, side):
        kv = jnp.dot(wbuf[g, 0 : 2 * rows, :], xbuf[side], preferred_element_type=f32)
        keys = jnp.maximum(kv[:rows].astype(bf16), jnp.zeros((), bf16))
        values = kv[rows:].astype(bf16)
        values = jnp.concatenate([values, jnp.ones((16, values.shape[1]), bf16)], axis=0)
        full = lax.dot_general(values, keys, (((1,), (1,)), ((), ())), preferred_element_type=f32)
        kept = jnp.where(same_head, full[:rows], 0.0)
        packed = kept[0:HEAD_DIM]
        for h in range(1, group_heads):
            packed = packed + kept[h * HEAD_DIM : (h + 1) * HEAD_DIM]
        st[side, g, 0:HEAD_DIM, :] = packed
        st[side, g, HEAD_DIM : HEAD_DIM + 8, :] = full[rows : rows + 8]

    def project(g, side):
        queries = jnp.dot(wbuf[g, 2 * rows : 3 * rows, :], xbuf[side], preferred_element_type=f32)
        qbuf[side, g] = jnp.maximum(queries, 0.0)

    def attend(g, side):
        queries = qbuf[side, g]
        q_hi = queries.astype(bf16)
        q_lo = (queries - q_hi.astype(f32)).astype(bf16)
        packed = total[side, g]
        numer = jnp.concatenate([packed[0:HEAD_DIM]] * group_heads, axis=0)
        denom = jnp.concatenate([packed[HEAD_DIM : HEAD_DIM + 8]] * (rows // 8), axis=0)
        state = jnp.concatenate(
            [jnp.where(same_head, numer, 0.0), jnp.where(same_head, denom, 0.0)], axis=0
        )
        s_hi = state.astype(bf16)
        s_lo = (state - s_hi.astype(f32)).astype(bf16)
        both = (
            jnp.dot(s_hi, q_hi, preferred_element_type=f32)
            + jnp.dot(s_hi, q_lo, preferred_element_type=f32)
            + jnp.dot(s_lo, q_hi, preferred_element_type=f32)
        )
        obuf[side, g] = (both[:rows] / (both[rows:] + EPSILON)).astype(bf16)

    def out_rows(g):
        return out.at[pl.ds(pl.multiple_of((2 * g + y) * rows, 16), rows), :]

    def out_local(g):
        return pltpu.make_async_copy(obuf.at[y, g], out_rows(g), o_local.at[g])

    def out_far(g):
        return pltpu.make_async_remote_copy(
            src_ref=obuf.at[1 - y, g], dst_ref=out_rows(g), send_sem=o_send.at[g],
            recv_sem=o_recv.at[g], device_id=facing, device_id_type=pl.DeviceIdType.MESH,
        )

    frame_local.wait()
    for copy in own_copies:
        copy.wait()

    def own_q(left_if, right_if):
        src = w_in.at[KIND_AT[Q]]

        @pl.when(primary & left_if)
        def _():
            w_copy(src, Q, z, z_send.at[0, Q, z], left).start()

        @pl.when(primary & right_if)
        def _():
            w_copy(src, Q, z, z_send.at[1, Q, z], right).start()

    for k in (1, 2, 3):
        for kind in (K, V):
            relay(kind, order[k])
        if k == 1:
            own_q(z >= 2, z < 2)
        if k == 3:
            own_q(z == 1, z == 2)
            relay(Q, order[1])
        for kind in (K, V):
            w_arrived(kind, order[k - 1], 1 - c)
        states(order[k - 1], y)
    for kind in (K, V):
        w_arrived(kind, order[3], 1 - c)
    states(order[3], y)
    frame_far.wait_recv()

    @pl.loop(0, 4)
    def _(g):
        states(g, 1 - y)

    swap = pltpu.make_async_remote_copy(
        src_ref=st, dst_ref=sib, send_sem=s_send, recv_sem=s_recv,
        device_id=sibling, device_id_type=pl.DeviceIdType.MESH,
    )
    swap.start()
    relay(Q, order[2])

    mine = pl.ds(2 * c, 2)
    onward = pltpu.make_async_remote_copy(
        src_ref=chain.at[mine], dst_ref=pre.at[mine], send_sem=c_send, recv_sem=c_recv,
        device_id=right, device_id_type=pl.DeviceIdType.MESH,
    )
    share = pltpu.make_async_remote_copy(
        src_ref=pre.at[mine], dst_ref=pre.at[mine], send_sem=h_send, recv_sem=h_recv,
        device_id=sibling, device_id_type=pl.DeviceIdType.MESH,
    )
    swap.wait_recv()
    near = st[0] + sib[0]
    later = jnp.where(c == 1, 1.0, 0.0).astype(f32)
    total[0] = st[0] + later * sib[0]
    total[1] = near + st[1] + later * sib[1]
    chain[...] = near + st[1] + sib[1]

    @pl.when(first)
    def _():
        onward.start()

    def project_both(g):
        w_arrived(Q, g, 1 - c)

        @pl.loop(0, 2)
        def _(side):
            project(g, side)

    project_both(order[0])
    relay(Q, order[3])

    @pl.when(jnp.logical_not(first))
    def _():
        pltpu.make_async_copy(pre.at[mine], pre.at[mine], c_recv).wait()

        @pl.when(jnp.logical_not(last))
        def _():
            chain[mine] = chain[mine] + pre[mine]
            onward.start()

        share.start()

    for k in (1, 2):
        project_both(order[k])

    @pl.when(jnp.logical_not(first))
    def _():
        share.wait_recv()
        total[0] = total[0] + pre[...]
        total[1] = total[1] + pre[...]

    def finish(g):
        attend(g, 1 - y)
        out_far(g).start()
        attend(g, y)
        out_local(g).start()

    for k in (0, 1, 2):
        attend(order[k], 1 - y)
        out_far(order[k]).start()
    project_both(order[3])
    attend(order[3], 1 - y)
    out_far(order[3]).start()
    for k in range(4):
        attend(order[k], y)
        out_local(order[k]).start()

    for kind in (K, V, Q):
        own_z(kind, sent)
        own_d(kind).wait_send()
        for k in (1, 2, 3):
            forward(kind, order[k], sent)
    frame_far.wait_send()
    swap.wait_send()

    @pl.when(jnp.logical_not(first))
    def _():
        share.wait_send()

    @pl.when(jnp.logical_not(last))
    def _():
        onward.wait_send()

    for g in range(4):
        out_local(g).wait()
        out_far(g).wait_send()
    for g in range(4):
        theirs = out.at[pl.ds(pl.multiple_of((2 * g + 1 - y) * rows, 16), rows), :]
        pltpu.make_async_copy(theirs, theirs, o_recv.at[g]).wait()


def kernel_shards(lines, frames_in, qkv_weight):
    tokens = jnp.swapaxes(frames_in[0], 0, 1)
    weights = jnp.swapaxes(qkv_weight, 1, 2)
    depth, count = tokens.shape
    half_rows = weights.shape[1]
    rows = 2 * half_rows
    dma = pltpu.SemaphoreType.DMA
    bf16, f32 = jnp.bfloat16, jnp.float32
    packed = (lines, HEAD_DIM + 8, rows)
    out = pl.pallas_call(
        functools.partial(kernel, lines),
        out_shape=jax.ShapeDtypeStruct((HEADS * HEAD_DIM, count), bf16),
        in_specs=[pl.BlockSpec(memory_space=pl.ANY)] * 2,
        out_specs=pl.BlockSpec(memory_space=pl.ANY),
        scratch_shapes=[
            pltpu.VMEM((lines, 3 * rows, depth), bf16),
            pltpu.VMEM((2, depth, count), bf16),
            pltpu.VMEM((2, lines, rows, count), f32),
            pltpu.VMEM((2, lines, rows, count), bf16),
            pltpu.VMEM((2,) + packed, f32),
            pltpu.VMEM((2,) + packed, f32),
            pltpu.VMEM((2,) + packed, f32),
            pltpu.VMEM(packed, f32),
            pltpu.VMEM(packed, f32),
            dma((3, lines, 2)),
            dma((2, 3, lines)),
            dma((3, lines)),
            dma((3, lines)),
            dma((3,)),
            dma, dma, dma, dma, dma, dma, dma, dma, dma,
            dma((lines,)),
            dma((lines,)),
            dma((lines,)),
        ],
        compiler_params=pltpu.CompilerParams(
            collective_id=0, has_side_effects=True, vmem_limit_bytes=63 * 1024 * 1024
        ),
    )(tokens, weights)
    return jnp.swapaxes(out, 0, 1)[None]


def solution(mesh):
    placed = (P(("groups", "frame"), None, None), P(None, None, "frame"))
    fits = mesh.shape["groups"] == 2 and mesh.shape["frame"] == 16
    shards = functools.partial(kernel_shards, mesh.shape["frame"] // 4) if fits else gathered_shards
    return jax.shard_map(
        shards,
        mesh=mesh,
        in_specs=placed,
        out_specs=P(("groups", "frame"), None, None),
        check_vma=False,
    )
```
